128 devices in a mesh: band: 32 (over x, z_lo, y), pw: 4 (over z_hi, core).
Axes of the slice: x: 4, y: 4, z: 4 (z_hi: 2, z_lo: 2; z = z_hi * 2 + z_lo), core: 2. Of those that a mesh axis runs over, the one named last changes fastest.
Arguments:
- cond_pairs: bfloat16 [256, 256, 5120], P('band', None, 'pw'), may hold values from -6 to 6
- vectors: bfloat16 [8, 24, 256], P(None, None, 'band'), may hold values from -0.375 to 0.375
- screened: bfloat16 [5120, 5120], P('pw', 'band'), may hold values from -0.078125 to 0.078125
- val_pairs: bfloat16 [256, 24, 5120], P('band', None, 'pw'), may hold values from -0.015625 to 0.015625
Outputs:
- sigma: float32 [8, 256, 256], P(None, 'pw', 'band')
The draws below stay inside these ranges and needn't reach their ends.
All inputs are finite; a program needn't handle non-finite values.
Results may differ from the reference program's by a relative error of at most 0.004.
Values may be sent and summed in bfloat16 or wider, within the bound.
No kernel may reach another device: no remote copies, remote signals or barrier semaphores. Data moves between devices by JAX's collectives and lax.ppermute only.
A program may use at most 192 MiB of HBM per device.

```python
import jax
import jax.numpy as jnp
from jax import lax

NV = 256
NC = 256
NG = 5120
VB = 24
NVEC = 8


def levels(rng, extent, shards, low, largest):
    factor_of, own = 1.0, jax.random.fold_in(rng, 6)
    for axis_at, blocks in shards:
        draws = jnp.exp(jax.random.uniform(jax.random.fold_in(own, axis_at), (blocks,), jnp.float32, low / len(shards), largest / len(shards)))
        factor_of = factor_of * jnp.repeat(draws, extent[axis_at] // blocks).reshape([-1 if axis == axis_at else 1 for axis in range(len(extent))])
    return factor_of


def scatter_about(own_key, shape, deviation, bound, pieces=(), held_as=jnp.bfloat16):
    level = levels(own_key, shape, pieces, -0.22, 0.18) if pieces else 1.0
    entries = jax.random.normal(own_key, shape, jnp.float32) * deviation * level
    return jnp.minimum(jnp.maximum(entries, -bound), bound).astype(held_as)


def setup_inputs(seed: int = 0) -> dict:
    streams_of = jax.random.split(jax.random.key(seed), 5)
    return {
        "cond_pairs": scatter_about(streams_of[0], (NC, NC, NG), 1.0, 6.0, ((0, 32), (2, 4))),
        "vectors": scatter_about(streams_of[1], (NVEC, VB, NC), NC ** -0.5, 0.375, ((2, 32),)),
        "screened": scatter_about(streams_of[2], (NG, NG), NG ** -0.5, 0.078125, ((0, 4), (1, 32))),
        "val_pairs": scatter_about(streams_of[3], (NV, VB, NG), (VB * NG) ** -0.5, 0.015625, ((0, 32), (2, 4))),
    }


def reference(cond_pairs, vectors, screened, val_pairs):
    rows = vectors.reshape(NVEC * VB, NC)
    flat = jnp.transpose(cond_pairs, (1, 0, 2)).reshape(NC, NC * NG)
    mixed = jnp.dot(rows, flat, preferred_element_type=jnp.float32).astype(jnp.bfloat16)
    mixed = mixed.reshape(NVEC * VB * NC, NG)
    applied = jnp.dot(mixed.astype(jnp.float32), screened.astype(jnp.float32).T, precision=lax.Precision.HIGHEST)
    applied = applied.astype(jnp.bfloat16).reshape(NVEC, VB, NC, NG)
    sigma = jnp.einsum("vwg,kwcg->kvc", val_pairs.astype(jnp.float32), applied.astype(jnp.float32), precision=lax.Precision.HIGHEST)
    return sigma
```

```python
import jax
import jax.numpy as jnp
from jax import lax
from jax.experimental import pallas as pl
from jax.experimental.pallas import tpu as pltpu
from jax.sharding import Mesh, PartitionSpec as P

F32, BF16 = jnp.float32, jnp.bfloat16
ANY = pl.BlockSpec(memory_space=pl.ANY)
SMEM = pl.BlockSpec(memory_space=pltpu.SMEM)
VMEM = pl.BlockSpec(memory_space=pltpu.VMEM)
VMEM_LIMIT = 56 * 1024 * 1024

NX, NY = 4, 4
NT = (((1,), (1,)), ((), ()))


def shift_from(a, axis, s):
    return lax.ppermute(a, axis, [(i, (i - s) % 4) for i in range(4)])


def shift_to(a, axis, s):
    return lax.ppermute(a, axis, [(i, (i + s) % 4) for i in range(4)])


def swap(a, axis):
    return lax.ppermute(a, axis, [(0, 1), (1, 0)])


def gather_zl_y(first, second):
    pair = jnp.stack([first, swap(first, "zl")])
    line = jnp.stack([second] + [shift_from(second, "y", s) for s in (1, 2, 3)])
    pairs = [pair] + [shift_from(pair, "y", s) for s in (1, 2, 3)]
    return pairs, [line, swap(line, "zl")]


def mixed_kernel(where, x_ref, b_ref, *refs):
    outs, xs, rows = refs[:4], refs[4], refs[5]

    @pl.when(pl.program_id(0) == 0)
    def _():
        x, zl, y = where[0], where[1], where[2]
        for at in range(32):
            z_of, x_of, y_of = at // 16, (at // 4) % 4, at % 4
            to = ((x + x_of) % 4) * 8 + (zl + z_of) % 2 * 4 + (y + y_of) % 4
            rows[pl.ds(pl.multiple_of(to * 8, 8), 8), :] = x_ref[at * 8 : at * 8 + 8, :]
        turned = rows[:, :].T
        rows2 = refs[6]
        rows2[...] = turned
        for j in range(4):
            q = (x + j) % 4
            xs[j * 48 : j * 48 + 48, :] = rows2[pl.ds(pl.multiple_of(q * 48, 48), 48), :].astype(BF16)

    lhs = xs[...]
    for pair in range(4):
        two = [jnp.dot(lhs, b_ref[2 * pair + i], preferred_element_type=F32) for i in range(2)]
        for j in range(4):
            for w in range(6):
                at = (j * 6 + w) * 8
                both = jnp.concatenate([t[at : at + 8] for t in two], axis=0)
                outs[j][w, 16 * pair : 16 * pair + 16, :] = both.astype(BF16)


def mix(where, x_all, cond):
    g = cond.shape[2]
    step = 256
    return pl.pallas_call(
        mixed_kernel,
        grid=(g // step,),
        in_specs=[
            SMEM,
            pl.BlockSpec((256, 192), lambda i: (0, 0)),
            pl.BlockSpec((8, 256, step), lambda i: (0, 0, i)),
        ],
        out_specs=[pl.BlockSpec((6, 64, step), lambda i: (0, 0, i))] * 4,
        out_shape=[jax.ShapeDtypeStruct((6, 64, g), BF16)] * 4,
        scratch_shapes=[pltpu.VMEM((192, 256), BF16), pltpu.VMEM((256, 192), F32), pltpu.VMEM((192, 256), F32)],
        compiler_params=pltpu.CompilerParams(vmem_limit_bytes=VMEM_LIMIT),
        cost_estimate=pl.CostEstimate(flops=2 * 192 * 256 * 8 * g, bytes_accessed=9200000, transcendentals=0),
        name="mix",
    )(where, x_all, cond)


def z_kernel(where, *refs):
    m, wa, wb = refs[0:4], refs[4:8], refs[8:10]
    send, keep, ms, ws, m_sem, w_sem = refs[10:]
    zl, y, zh, core = where[1], where[2], where[3], where[4]
    copies = []
    for t in range(4):
        owner = 1 - core if t < 2 else core
        q = 2 * owner + (zh + t % 2) % 2
        for r in range(4):
            copies.append(
                pltpu.make_async_copy(
                    m[r].at[pl.ds(pl.multiple_of(q * 48, 48), 48)], ms.at[t, pl.ds(48 * r, 48)], m_sem.at[t * 4 + r]
                )
            )
    for z_of in range(2):
        for y_of in range(4):
            to = ((zl + z_of) % 2 * 4 + (y + y_of) % 4) * 160
            at = z_of * 4 + y_of
            copies.append(
                pltpu.make_async_copy(
                    wa[y_of].at[z_of], ws.at[pl.ds(pl.multiple_of(to, 160), 80)], w_sem.at[at]
                )
            )
            copies.append(
                pltpu.make_async_copy(
                    wb[z_of].at[y_of], ws.at[pl.ds(pl.multiple_of(to + 80, 80), 80)], w_sem.at[8 + at]
                )
            )
    for c in copies:
        c.start()
    for c in copies:
        c.wait()

    for half, out in enumerate((send, keep)):

        @pl.loop(0, 2)
        def _(a, half=half, out=out):
            lhs = ms[2 * half + a]
            for n in range(5):
                cols = slice(256 * n, 256 * n + 256)
                res = lax.dot_general(lhs, ws[cols, :], NT, preferred_element_type=F32)
                for w in range(6):
                    for r in range(4):
                        at = (r * 6 + w) * 8
                        out[a, (w * 4 + r) * 8 : (w * 4 + r) * 8 + 8, cols] = res[at : at + 8]


def make_z(where, m, wa, wb):
    g = m[0].shape[1]
    shape = jax.ShapeDtypeStruct((2, 192, g), F32)
    return pl.pallas_call(
        z_kernel,
        in_specs=[SMEM] + [ANY] * 10,
        out_specs=[VMEM, VMEM],
        out_shape=[shape, shape],
        scratch_shapes=[
            pltpu.VMEM((4, 192, g), BF16),
            pltpu.VMEM((g, g), BF16),
            pltpu.SemaphoreType.DMA((16,)),
            pltpu.SemaphoreType.DMA((16,)),
        ],
        compiler_params=pltpu.CompilerParams(vmem_limit_bytes=VMEM_LIMIT),
        cost_estimate=pl.CostEstimate(flops=2 * 768 * g * g, bytes_accessed=9000000, transcendentals=0),
        name="make_z",
    )(where, *m, *wa, *wb)


def last_kernel(where, *refs):
    za, zb, mx = refs[0:4], refs[4:6], refs[6:10]
    out, zs, xs, total, sem = refs[10:]
    zl, y = where[1], where[2]
    copies = []
    for z_of in range(2):
        for y_of in range(4):
            at = z_of * 4 + y_of
            copies.append(pltpu.make_async_copy(za[y_of].at[z_of], zs.at[pl.ds(0, 3), at], sem.at[at]))
            copies.append(pltpu.make_async_copy(zb[z_of].at[y_of], zs.at[pl.ds(3, 3), at], sem.at[8 + at]))
    for j in range(4):
        copies.append(pltpu.make_async_copy(mx[j], xs.at[:, j], sem.at[16 + j]))
    for c in copies:
        c.start()
    for c in copies:
        c.wait()
    sums = jnp.zeros((256, 256), F32)
    for w in range(6):
        lhs = zs[w].reshape(256, zs.shape[3])
        rhs = xs[w].reshape(256, xs.shape[3])
        sums = sums + lax.dot_general(lhs, rhs, NT, preferred_element_type=F32)
    for z_of in range(2):
        for y_of in range(4):
            to = ((zl + z_of) % 2 * 4 + (y + y_of) % 4) * 8
            for r in range(4):
                at = ((z_of * 4 + y_of) * 4 + r) * 8
                total[pl.ds(pl.multiple_of(r * 64 + to, 8), 8), :] = sums[at : at + 8]
    turned = total[...].T
    for j in range(4):
        out[j] = turned[64 * j : 64 * j + 64]


def last(where, za, zb, mixed):
    g = mixed[0].shape[2]
    return pl.pallas_call(
        last_kernel,
        in_specs=[SMEM] + [ANY] * 10,
        out_specs=VMEM,
        out_shape=jax.ShapeDtypeStruct((4, 64, 256), F32),
        scratch_shapes=[
            pltpu.VMEM((6, 8, 32, g), BF16),
            pltpu.VMEM((6, 4, 64, g), BF16),
            pltpu.VMEM((256, 256), F32),
            pltpu.SemaphoreType.DMA((20,)),
        ],
        compiler_params=pltpu.CompilerParams(vmem_limit_bytes=VMEM_LIMIT),
        cost_estimate=pl.CostEstimate(flops=2 * 256 * 256 * 6 * g, bytes_accessed=8000000, transcendentals=0),
        name="last",
    )(where, *za, *zb, *mixed)


def shards(cond_pairs, vectors, screened, val_pairs):
    g = cond_pairs.shape[2]
    axes = ("x", "zl", "y", "zh", "core")
    where = jnp.stack([lax.axis_index(a) for a in axes]).astype(jnp.int32)

    own = jnp.transpose(vectors, (2, 1, 0)).reshape(8, 192).astype(F32)
    by_y = jnp.concatenate([own] + [shift_from(own, "y", s) for s in (1, 2, 3)])
    by_x = jnp.concatenate([by_y] + [shift_from(by_y, "x", s) for s in (1, 2, 3)])
    x_all = jnp.concatenate([by_x, swap(by_x, "zl")])

    w_t = screened.T
    wa, wb = gather_zl_y(w_t[:80], w_t[80:])
    m_own = jnp.transpose(val_pairs, (1, 0, 2)).reshape(192, g)
    m = [m_own] + [shift_from(m_own, "x", s) for s in (1, 2, 3)]

    mixed = mix(where, x_all, cond_pairs)
    mixed = [mixed[0]] + [shift_to(mixed[j], "x", j) for j in (1, 2, 3)]

    send, keep = make_z(where, m, wa, wb)
    part = (keep + swap(send, "core")).astype(BF16)
    got = []
    for a in range(2):
        perm = [
            (x * 4 + zh * 2 + c, (2 * c + (zh ^ a)) * 4 + x) for x in range(4) for zh in range(2) for c in range(2)
        ]
        got.append(lax.ppermute(part[a], ("x", "zh", "core"), perm))
    z = (got[0].astype(F32) + got[1].astype(F32)).astype(BF16).reshape(2, 3, 32, g)
    za, zb = gather_zl_y(z[0], z[1])

    sums = last(where, za, zb, mixed)
    over_x = sums[0]
    for j in (1, 2, 3):
        over_x = over_x + shift_from(sums[j], "x", j)
    total = over_x[:, :64]
    for r in (1, 2, 3):
        total = total + shift_to(over_x[:, 64 * r : 64 * r + 64], ("zh", "core"), r)
    return jnp.transpose(total.reshape(8, 8, 64), (1, 2, 0))


def solution(mesh):
    fine = Mesh(mesh.devices.reshape(4, 2, 4, 2, 2), ("x", "zl", "y", "zh", "core"))
    band, pw = ("x", "zl", "y"), ("zh", "core")
    return jax.shard_map(
        shards,
        mesh=fine,
        in_specs=(P(band, None, pw), P(None, None, band), P(pw, band), P(band, None, pw)),
        out_specs=P(None, pw, band),
        check_vma=False,
    )
```

```python
import jax
import jax.numpy as jnp
from jax import lax
from jax.experimental import pallas as pl
from jax.experimental.pallas import tpu as pltpu
from jax.sharding import Mesh, PartitionSpec as P

F32, BF16 = jnp.float32, jnp.bfloat16
ANY = pl.BlockSpec(memory_space=pl.ANY)
SMEM = pl.BlockSpec(memory_space=pltpu.SMEM)
VMEM = pl.BlockSpec(memory_space=pltpu.VMEM)
VMEM_LIMIT = 56 * 1024 * 1024

NX, NY = 4, 4
NT = (((1,), (1,)), ((), ()))


def shift_from(a, axis, s):
    return lax.ppermute(a, axis, [(i, (i - s) % 4) for i in range(4)])


def shift_to(a, axis, s):
    return lax.ppermute(a, axis, [(i, (i + s) % 4) for i in range(4)])


def swap(a, axis):
    return lax.ppermute(a, axis, [(0, 1), (1, 0)])


def start_gather(own):
    return swap(own, "zl"), shift_from(own, "y", 1), shift_from(own, "y", 3), shift_from(own, "y", 2)


def end_gather(own, other, one, three, two):
    other_two = swap(two, "zl")
    other_one, other_three = shift_from(other, "y", 1), shift_from(other, "y", 3)
    return [own, one, two, three, other, other_one, other_two, other_three]


def mixed_kernel(where, x_ref, b_ref, *refs):
    outs, xs, rows = refs[:4], refs[4], refs[5]

    @pl.when(pl.program_id(0) == 0)
    def _():
        x = where[0]
        rows[...] = x_ref[...].T
        for j in range(4):
            q = (x + j) % 4
            xs[j * 48 : j * 48 + 48, :] = rows[pl.ds(pl.multiple_of(q * 48, 48), 48), :].astype(BF16)

    lhs = xs[...]
    for pair in range(4):
        two = [jnp.dot(lhs, b_ref[2 * pair + i], preferred_element_type=F32) for i in range(2)]
        for j in range(4):
            for w in range(6):
                at = (j * 6 + w) * 8
                both = jnp.concatenate([t[at : at + 8] for t in two], axis=0)
                outs[j][w, 16 * pair : 16 * pair + 16, :] = both.astype(BF16)


def mix(where, x_all, cond):
    g = cond.shape[2]
    step = 256
    return pl.pallas_call(
        mixed_kernel,
        grid=(g // step,),
        in_specs=[
            SMEM,
            pl.BlockSpec((256, 192), lambda i: (0, 0)),
            pl.BlockSpec((8, 256, step), lambda i: (0, 0, i)),
        ],
        out_specs=[pl.BlockSpec((6, 64, step), lambda i: (0, 0, i))] * 4,
        out_shape=[jax.ShapeDtypeStruct((6, 64, g), BF16)] * 4,
        scratch_shapes=[pltpu.VMEM((192, 256), BF16), pltpu.VMEM((192, 256), F32)],
        compiler_params=pltpu.CompilerParams(vmem_limit_bytes=VMEM_LIMIT),
        cost_estimate=pl.CostEstimate(flops=2 * 192 * 256 * 8 * g, bytes_accessed=9200000, transcendentals=0),
        name="mix",
    )(where, x_all, cond)


def z_kernel(where, m, *refs):
    w = refs[0:8]
    send, keep, ms, ws, m_sem, w_sem = refs[8:]
    zl, y, zh, core = where[1], where[2], where[3], where[4]
    copies = []
    for t in range(4):
        owner = 1 - core if t < 2 else core
        q = 2 * owner + (zh + t % 2) % 2
        for r in range(4):
            to = ms.at[t // 2, pl.ds((t % 2 * 4 + r) * 48, 48)]
            at = pl.ds(pl.multiple_of(192 * r + q * 48, 48), 48)
            copies.append(pltpu.make_async_copy(m.at[at], to, m_sem.at[t * 4 + r]))
    for at in range(8):
        to = ((zl + at // 4) % 2 * 4 + (y + at % 4) % 4) * 160
        copies.append(pltpu.make_async_copy(w[at], ws.at[pl.ds(pl.multiple_of(to, 160), 160)], w_sem.at[at]))
    for c in copies:
        c.start()
    for c in copies:
        c.wait()

    for half, out in enumerate((send, keep)):

        @pl.loop(0, 5)
        def _(n, half=half, out=out):
            cols = pl.ds(pl.multiple_of(256 * n, 256), 256)
            res = lax.dot_general(ms[half], ws[cols, :], NT, preferred_element_type=F32)
            for a in range(2):
                for w in range(6):
                    for r in range(4):
                        at = ((a * 4 + r) * 6 + w) * 8
                        out[a, (w * 4 + r) * 8 : (w * 4 + r) * 8 + 8, cols] = res[at : at + 8]


def make_z(where, m, w):
    g = m.shape[1]
    shape = jax.ShapeDtypeStruct((2, 192, g), F32)
    return pl.pallas_call(
        z_kernel,
        in_specs=[SMEM] + [ANY] * 9,
        out_specs=[VMEM, VMEM],
        out_shape=[shape, shape],
        scratch_shapes=[
            pltpu.VMEM((2, 384, g), BF16),
            pltpu.VMEM((g, g), BF16),
            pltpu.SemaphoreType.DMA((16,)),
            pltpu.SemaphoreType.DMA((8,)),
        ],
        compiler_params=pltpu.CompilerParams(vmem_limit_bytes=VMEM_LIMIT),
        cost_estimate=pl.CostEstimate(flops=2 * 768 * g * g, bytes_accessed=9000000, transcendentals=0),
        name="make_z",
    )(where, m, *w)


def last_kernel(where, *refs):
    z, mx = refs[0:8], refs[8:12]
    out, zs, xs, total, sem = refs[12:]
    x, zl, y = where[0], where[1], where[2]
    copies = []
    for at in range(8):
        copies.append(pltpu.make_async_copy(z[at], zs.at[:, at], sem.at[at]))
    for j in range(4):
        copies.append(pltpu.make_async_copy(mx[j], xs.at[:, (x + 4 - j) % 4], sem.at[8 + j]))
    for c in copies:
        c.start()
    for c in copies:
        c.wait()
    sums = jnp.zeros((256, 256), F32)
    for w in range(6):
        lhs = zs[w].reshape(256, zs.shape[3])
        rhs = xs[w].reshape(256, xs.shape[3])
        sums = sums + lax.dot_general(lhs, rhs, NT, preferred_element_type=F32)
    for z_of in range(2):
        for y_of in range(4):
            to = ((zl + z_of) % 2 * 4 + (y + y_of) % 4) * 8
            for r in range(4):
                at = ((z_of * 4 + y_of) * 4 + r) * 8
                total[pl.ds(pl.multiple_of(r * 64 + to, 8), 8), :] = sums[at : at + 8]
    turned = total[...].T
    for j in range(4):
        for p in range(4):
            cols = slice(64 * p, 64 * p + 64)
            halves = [turned[64 * j + at : 64 * j + at + 32, cols] for at in (0, 32)]
            out[4 * j + p] = jnp.concatenate(halves, axis=1)


def last(where, z, mixed):
    g = mixed[0].shape[2]
    return pl.pallas_call(
        last_kernel,
        in_specs=[SMEM] + [ANY] * 12,
        out_specs=VMEM,
        out_shape=jax.ShapeDtypeStruct((16, 32, 128), F32),
        scratch_shapes=[
            pltpu.VMEM((6, 8, 32, g), BF16),
            pltpu.VMEM((6, 4, 64, g), BF16),
            pltpu.VMEM((256, 256), F32),
            pltpu.SemaphoreType.DMA((12,)),
        ],
        compiler_params=pltpu.CompilerParams(vmem_limit_bytes=VMEM_LIMIT),
        cost_estimate=pl.CostEstimate(flops=2 * 256 * 256 * 6 * g, bytes_accessed=8000000, transcendentals=0),
        name="last",
    )(where, *z, *mixed)


def shards(cond_pairs, vectors, screened, val_pairs):
    g = cond_pairs.shape[2]
    axes = ("x", "zl", "y", "zh", "core")
    where = jnp.stack([lax.axis_index(a) for a in axes]).astype(jnp.int32)

    m_own = jnp.transpose(val_pairs, (1, 0, 2)).reshape(192, g)
    m = lax.all_gather(m_own, "x", axis=0, tiled=True)

    w_own = screened.T
    w = start_gather(w_own)

    own = jnp.transpose(vectors, (2, 1, 0)).reshape(1, 8, 192).astype(F32)
    x_all = lax.all_to_all(jnp.broadcast_to(own, (32, 8, 192)), ("x", "zl", "y"), split_axis=0, concat_axis=0, tiled=True)

    w, x_all = lax.optimization_barrier((w, x_all.reshape(256, 192)))
    w = end_gather(w_own, *w)
    mixed = mix(where, x_all, cond_pairs)
    m, w, mixed = lax.optimization_barrier((m, w, list(mixed)))
    mixed[1], mixed[3] = shift_to(mixed[1], "x", 1), shift_to(mixed[3], "x", 3)

    send, keep = make_z(where, m, w)
    part = (keep + swap(send, "core")).astype(BF16)
    got = []
    for a in range(2):
        perm = [
            (x * 4 + zh * 2 + c, (2 * c + (zh ^ a)) * 4 + x) for x in range(4) for zh in range(2) for c in range(2)
        ]
        got.append(lax.ppermute(part[a], ("x", "zh", "core"), perm))
    got, mixed = lax.optimization_barrier((got, mixed))
    mixed[2] = shift_to(mixed[2], "x", 2)
    z_own = (got[0].astype(F32) + got[1].astype(F32)).astype(BF16).reshape(6, 32, g)
    z = end_gather(z_own, *start_gather(z_own))

    sums = last(where, z, mixed)
    sums = lax.all_to_all(sums, ("x", "zh", "core"), split_axis=0, concat_axis=0, tiled=True)
    total = jnp.sum(sums, axis=0)
    total = jnp.stack([total[:, :64], total[:, 64:]])
    return jnp.transpose(total.reshape(8, 8, 64), (1, 2, 0))


def solution(mesh):
    fine = Mesh(mesh.devices.reshape(4, 2, 4, 2, 2), ("x", "zl", "y", "zh", "core"))
    band, pw = ("x", "zl", "y"), ("zh", "core")
    return jax.shard_map(
        shards,
        mesh=fine,
        in_specs=(P(band, None, pw), P(None, None, band), P(pw, band), P(band, None, pw)),
        out_specs=P(None, pw, band),
        check_vma=False,
    )
```

```python
import jax
import jax.numpy as jnp
from jax import lax
from jax.experimental import pallas as pl
from jax.experimental.pallas import tpu as pltpu
from jax.sharding import Mesh, PartitionSpec as P

F32, BF16 = jnp.float32, jnp.bfloat16
ANY = pl.BlockSpec(memory_space=pl.ANY)
SMEM = pl.BlockSpec(memory_space=pltpu.SMEM)
VMEM = pl.BlockSpec(memory_space=pltpu.VMEM)
VMEM_LIMIT = 60 * 1024 * 1024

NX, NY = 4, 4
NT = (((1,), (1,)), ((), ()))


def shift_from(a, axis, s):
    return lax.ppermute(a, axis, [(i, (i - s) % 4) for i in range(4)])


def shift_to(a, axis, s):
    return lax.ppermute(a, axis, [(i, (i + s) % 4) for i in range(4)])


def swap(a, axis):
    return lax.ppermute(a, axis, [(0, 1), (1, 0)])


def end_gather(own, other, two):
    pair = jnp.stack([own, other])
    return [own, other, two, swap(two, "zl"), shift_from(pair, "y", 1), shift_from(pair, "y", 3)]


def blocks_of(refs):
    own, other, two, other_two, one, three = refs
    return [own, one.at[0], two, three.at[0], other, one.at[1], other_two, three.at[1]]


def mixed_kernel(where, x_ref, b_ref, *refs):
    outs, xs, rows = refs[:6], refs[6], refs[7]

    @pl.when(pl.program_id(0) == 0)
    def _():
        x = where[0]
        rows[...] = x_ref[...].astype(F32).T
        for j in range(4):
            q = (x + j) % 4
            xs[j * 48 : j * 48 + 48, :] = rows[pl.ds(pl.multiple_of(q * 48, 48), 48), :].astype(BF16)

    lhs = xs[...]
    for n in range(b_ref.shape[2] // 256):
        cols = slice(256 * n, 256 * n + 256)
        two = [jnp.dot(lhs, b_ref[i, :, cols], preferred_element_type=F32) for i in range(2)]
        for j in range(4):
            for w in range(6):
                at = (j * 6 + w) * 8
                both = jnp.concatenate([t[at : at + 8] for t in two], axis=0)
                if j % 2:
                    outs[j + 1 + w // 3][w % 3, :, cols] = both.astype(BF16)
                else:
                    outs[j // 2][w, :, cols] = both.astype(BF16)


def mix(where, x_all, cond):
    g = cond.shape[2]
    return pl.pallas_call(
        mixed_kernel,
        grid=(4,),
        in_specs=[
            SMEM,
            pl.BlockSpec((256, 192), lambda i: (0, 0)),
            pl.BlockSpec((2, 256, g), lambda i: (i, 0, 0)),
        ],
        out_specs=[pl.BlockSpec((6, 16, g), lambda i: (0, i, 0))] * 2
        + [pl.BlockSpec((3, 16, g), lambda i: (0, i, 0))] * 4,
        out_shape=[jax.ShapeDtypeStruct((6, 64, g), BF16)] * 2 + [jax.ShapeDtypeStruct((3, 64, g), BF16)] * 4,
        scratch_shapes=[pltpu.VMEM((192, 256), BF16), pltpu.VMEM((192, 256), F32)],
        compiler_params=pltpu.CompilerParams(vmem_limit_bytes=VMEM_LIMIT),
        cost_estimate=pl.CostEstimate(flops=2 * 192 * 256 * 8 * g, bytes_accessed=9200000, transcendentals=0),
        name="mix",
    )(where, x_all, cond)


def z_kernel(where, m, *refs):
    w = blocks_of(refs[0:6])
    send, keep, ms, ws, sums, m_sem, w_sem, out_sem = refs[6:]
    zl, y, zh, core = where[1], where[2], where[3], where[4]
    copies = []
    for t in range(4):
        owner = 1 - core if t < 2 else core
        q = 2 * owner + (zh + t % 2) % 2
        for r in range(4):
            to = ms.at[pl.ds((t * 4 + r) * 48, 48)]
            at = pl.ds(pl.multiple_of(192 * r + q * 48, 48), 48)
            copies.append(pltpu.make_async_copy(m.at[at], to, m_sem.at[t * 4 + r]))
    for c in copies:
        c.start()
    for at in range(8):
        to = (zl + at // 4) % 2 * 4 + (y + at % 4) % 4
        pltpu.make_async_copy(w[at], ws.at[pl.ds(pl.multiple_of(to * 160, 160), 160)], w_sem.at[to]).start()
    for c in copies:
        c.wait()

    for i in range(8):
        pltpu.make_async_copy(w[0], ws.at[pl.ds(i * 160, 160)], w_sem.at[i]).wait()
    outs = []
    for half, out in enumerate((send, keep)):
        res = lax.dot_general(ms[384 * half : 384 * half + 384, :], ws[...], NT, preferred_element_type=F32)
        for a in range(2):
            t = 2 * half + a
            for k in range(6):
                for r in range(4):
                    at = ((a * 4 + r) * 6 + k) * 8
                    sums[t, (k * 4 + r) * 8 : (k * 4 + r) * 8 + 8, :] = res[at : at + 8]
            outs.append(pltpu.make_async_copy(sums.at[t], out.at[a], out_sem.at[t]))
            outs[-1].start()
    for c in outs:
        c.wait()


def make_z(where, m, w):
    g = m.shape[1]
    shape = jax.ShapeDtypeStruct((2, 192, g), F32)
    return pl.pallas_call(
        z_kernel,
        in_specs=[SMEM] + [ANY] * 7,
        out_specs=[ANY, ANY],
        out_shape=[shape, shape],
        scratch_shapes=[
            pltpu.VMEM((768, g), BF16),
            pltpu.VMEM((g, g), BF16),
            pltpu.VMEM((4, 192, g), F32),
            pltpu.SemaphoreType.DMA((16,)),
            pltpu.SemaphoreType.DMA((8,)),
            pltpu.SemaphoreType.DMA((4,)),
        ],
        compiler_params=pltpu.CompilerParams(vmem_limit_bytes=VMEM_LIMIT),
        cost_estimate=pl.CostEstimate(flops=2 * 768 * g * g, bytes_accessed=40000000, transcendentals=0),
        name="make_z",
    )(where, m, *w)


def last_kernel(where, *refs):
    z, mx = blocks_of(refs[0:6]), refs[6:12]
    out, zs, xs, total, sem = refs[12:]
    x, zl, y = where[0], where[1], where[2]
    thirds = [[], [], []]
    for third in range(3):
        part = pl.ds(2 * third, 2)
        for at in range(8):
            thirds[third].append(pltpu.make_async_copy(z[at].at[part], zs.at[part, at], sem.at[third, at]))
        for j in (0, 2):
            to = xs.at[part, (x + 4 - j) % 4]
            thirds[third].append(pltpu.make_async_copy(mx[j // 2].at[part], to, sem.at[third, 8 + j]))
        for j in (1, 3):
            to = (x + 4 - j) % 4
            for w in range(2 * third, 2 * third + 2):
                own = mx[j + 1 + w // 3].at[w % 3]
                thirds[third].append(pltpu.make_async_copy(own, xs.at[w, to], sem.at[third, 8 + j + 4 * (w % 2)]))
        for c in thirds[third]:
            c.start()
    sums = jnp.zeros((256, 256), F32)
    for third in range(3):
        for c in thirds[third]:
            c.wait()
        for w in range(2 * third, 2 * third + 2):
            lhs = zs[w].reshape(256, zs.shape[3])
            rhs = xs[w].reshape(256, xs.shape[3])
            sums = sums + lax.dot_general(lhs, rhs, NT, preferred_element_type=F32)
    for z_of in range(2):
        for y_of in range(4):
            to = ((zl + z_of) % 2 * 4 + (y + y_of) % 4) * 8
            for r in range(4):
                at = ((z_of * 4 + y_of) * 4 + r) * 8
                total[pl.ds(pl.multiple_of(r * 64 + to, 8), 8), :] = sums[at : at + 8]
    turned = total[...].T
    for j in range(4):
        for p in range(4):
            cols = slice(64 * p, 64 * p + 64)
            halves = [turned[64 * j + at : 64 * j + at + 32, cols] for at in (0, 32)]
            out[4 * j + p] = jnp.concatenate(halves, axis=1)


def last(where, z, mixed):
    g = mixed[0].shape[2]
    return pl.pallas_call(
        last_kernel,
        in_specs=[SMEM] + [ANY] * 12,
        out_specs=VMEM,
        out_shape=jax.ShapeDtypeStruct((16, 32, 128), F32),
        scratch_shapes=[
            pltpu.VMEM((6, 8, 32, g), BF16),
            pltpu.VMEM((6, 4, 64, g), BF16),
            pltpu.VMEM((256, 256), F32),
            pltpu.SemaphoreType.DMA((3, 16)),
        ],
        compiler_params=pltpu.CompilerParams(vmem_limit_bytes=VMEM_LIMIT),
        cost_estimate=pl.CostEstimate(flops=2 * 256 * 256 * 6 * g, bytes_accessed=8000000, transcendentals=0),
        name="last",
    )(where, *z, *mixed)


def shards(cond_pairs, vectors, screened, val_pairs):
    g = cond_pairs.shape[2]
    axes = ("x", "zl", "y", "zh", "core")
    where = jnp.stack([lax.axis_index(a) for a in axes]).astype(jnp.int32)

    m_own = jnp.transpose(val_pairs, (1, 0, 2)).reshape(192, g)
    m = lax.all_gather(m_own, "x", axis=0, tiled=True)

    w_own = screened.T
    other, two = swap(w_own, "zl"), shift_from(w_own, "y", 2)

    own = jnp.transpose(vectors, (2, 1, 0)).reshape(1, 8, 192)
    line = lax.all_to_all(jnp.broadcast_to(own, (4, 8, 192)), "y", split_axis=0, concat_axis=0, tiled=True)
    other, two, line = lax.optimization_barrier((other, two, line))
    w = end_gather(w_own, other, two)
    lines = jnp.broadcast_to(line.reshape(1, 32, 192), (8, 32, 192))
    x_all = lax.all_to_all(lines, ("x", "zl"), split_axis=0, concat_axis=0, tiled=True).reshape(256, 192)

    mixed = mix(where, x_all, cond_pairs)
    mixed = list(mixed)
    m, w, mixed[0] = lax.optimization_barrier((m, w, mixed[0]))
    mixed[2], mixed[4] = shift_to(mixed[2], "x", 1), shift_to(mixed[4], "x", 3)

    send, keep = make_z(where, m, w)
    send, keep, mixed = lax.optimization_barrier((send, keep, mixed))
    part = (keep + swap(send, "core")).astype(BF16)
    got = []
    for a in range(2):
        perm = [
            (x * 4 + zh * 2 + c, (2 * c + (zh ^ a)) * 4 + x) for x in range(4) for zh in range(2) for c in range(2)
        ]
        got.append(lax.ppermute(part[a], ("x", "zh", "core"), perm))
    got, mixed = lax.optimization_barrier((got, mixed))
    z_own = (got[0].astype(F32) + got[1].astype(F32)).astype(BF16).reshape(6, 32, g)
    other, two = swap(z_own, "zl"), shift_from(z_own, "y", 2)
    mixed[3], mixed[5] = shift_to(mixed[3], "x", 1), shift_to(mixed[5], "x", 3)
    z_own, other, two, mixed = lax.optimization_barrier((z_own, other, two, mixed))
    z = end_gather(z_own, other, two)
    mixed[1] = shift_to(mixed[1], "x", 2)

    sums = last(where, z, mixed)
    sums = lax.all_to_all(sums, ("x", "zh", "core"), split_axis=0, concat_axis=0, tiled=True)
    total = jnp.sum(sums, axis=0)
    total = jnp.stack([total[:, :64], total[:, 64:]])
    return jnp.transpose(total.reshape(8, 8, 64), (1, 2, 0))


def solution(mesh):
    fine = Mesh(mesh.devices.reshape(4, 2, 4, 2, 2), ("x", "zl", "y", "zh", "core"))
    band, pw = ("x", "zl", "y"), ("zh", "core")
    return jax.shard_map(
        shards,
        mesh=fine,
        in_specs=(P(band, None, pw), P(None, None, band), P(pw, band), P(band, None, pw)),
        out_specs=P(None, pw, band),
        check_vma=False,
    )
```

```python
import jax
import jax.numpy as jnp
from jax import lax
from jax.experimental import pallas as pl
from jax.experimental.pallas import tpu as pltpu
from jax.sharding import Mesh, PartitionSpec as P

F32, BF16 = jnp.float32, jnp.bfloat16
ANY = pl.BlockSpec(memory_space=pl.ANY)
SMEM = pl.BlockSpec(memory_space=pltpu.SMEM)
VMEM = pl.BlockSpec(memory_space=pltpu.VMEM)
VMEM_LIMIT = 60 * 1024 * 1024

NX, NY = 4, 4
NT = (((1,), (1,)), ((), ()))


def shift_from(a, axis, s):
    return lax.ppermute(a, axis, [(i, (i - s) % 4) for i in range(4)])


def shift_to(a, axis, s):
    return lax.ppermute(a, axis, [(i, (i + s) % 4) for i in range(4)])


def swap(a, axis):
    return lax.ppermute(a, axis, [(0, 1), (1, 0)])


def end_gather(own, other, two):
    pair = jnp.stack([own, other])
    return [own, other, two, swap(two, "zl"), shift_from(pair, "y", 1), shift_from(pair, "y", 3)]


def blocks_of(refs):
    own, other, two, other_two, one, three = refs
    return [own, one.at[0], two, three.at[0], other, one.at[1], other_two, three.at[1]]


def mixed_kernel(where, x_ref, b_ref, *refs):
    outs, xs, rows, square = refs[:6], refs[6], refs[7], refs[8]

    @pl.when(pl.program_id(0) == 0)
    def _():
        x, y = where[0], where[2]
        given = x_ref[...].astype(F32)
        for at in range(32):
            to = at // 4 * 32 + (y + at % 4) % 4 * 8
            square[pl.ds(pl.multiple_of(to, 8), 8), :] = given[at * 8 : at * 8 + 8]
        rows[...] = square[...].T
        for j in range(4):
            q = (x + j) % 4
            xs[j * 48 : j * 48 + 48, :] = rows[pl.ds(pl.multiple_of(q * 48, 48), 48), :].astype(BF16)

    lhs = xs[...]
    for n in range(b_ref.shape[2] // 256):
        cols = slice(256 * n, 256 * n + 256)
        two = [jnp.dot(lhs, b_ref[i, :, cols], preferred_element_type=F32) for i in range(2)]
        for j in range(4):
            for w in range(6):
                at = (j * 6 + w) * 8
                both = jnp.concatenate([t[at : at + 8] for t in two], axis=0)
                if j % 2:
                    outs[j + 1 + w // 3][w % 3, :, cols] = both.astype(BF16)
                else:
                    outs[j // 2][w, :, cols] = both.astype(BF16)


def mix(where, x_all, cond):
    g = cond.shape[2]
    return pl.pallas_call(
        mixed_kernel,
        grid=(4,),
        in_specs=[
            SMEM,
            pl.BlockSpec((256, 192), lambda i: (0, 0)),
            pl.BlockSpec((2, 256, g), lambda i: (i, 0, 0)),
        ],
        out_specs=[pl.BlockSpec((6, 16, g), lambda i: (0, i, 0))] * 2
        + [pl.BlockSpec((n, 16, g), lambda i: (0, i, 0)) for n in (3, 3, 3, 3)],
        out_shape=[jax.ShapeDtypeStruct((n, 64, g), BF16) for n in (6, 6, 3, 3, 3, 3)],
        scratch_shapes=[pltpu.VMEM((192, 256), BF16), pltpu.VMEM((192, 256), F32), pltpu.VMEM((256, 192), F32)],
        compiler_params=pltpu.CompilerParams(vmem_limit_bytes=VMEM_LIMIT),
        cost_estimate=pl.CostEstimate(flops=2 * 192 * 256 * 8 * g, bytes_accessed=9200000, transcendentals=0),
        name="mix",
    )(where, x_all, cond)


def z_kernel(where, m, *refs):
    w = blocks_of(refs[0:6])
    send, keep, ms, ws, sums, m_sem, w_sem, out_sem = refs[6:]
    zl, y, zh, core = where[1], where[2], where[3], where[4]
    copies = []
    for t in range(4):
        owner = 1 - core if t < 2 else core
        q = 2 * owner + (zh + t % 2) % 2
        for r in range(4):
            to = ms.at[pl.ds((t * 4 + r) * 48, 48)]
            at = pl.ds(pl.multiple_of(192 * r + q * 48, 48), 48)
            copies.append(pltpu.make_async_copy(m.at[at], to, m_sem.at[t * 4 + r]))
    for c in copies:
        c.start()
    for at in range(8):
        to = (zl + at // 4) % 2 * 4 + (y + at % 4) % 4
        pltpu.make_async_copy(w[at], ws.at[pl.ds(pl.multiple_of(to * 160, 160), 160)], w_sem.at[to]).start()
    for c in copies:
        c.wait()

    for i in range(8):
        pltpu.make_async_copy(w[0], ws.at[pl.ds(i * 160, 160)], w_sem.at[i]).wait()
    outs = []
    for half, out in enumerate((send, keep)):
        res = lax.dot_general(ms[384 * half : 384 * half + 384, :], ws[...], NT, preferred_element_type=F32)
        for a in range(2):
            t = 2 * half + a
            for k in range(6):
                for r in range(4):
                    at = ((a * 4 + r) * 6 + k) * 8
                    sums[t, (k * 4 + r) * 8 : (k * 4 + r) * 8 + 8, :] = res[at : at + 8]
            outs.append(pltpu.make_async_copy(sums.at[t], out.at[a], out_sem.at[t]))
            outs[-1].start()
    for c in outs:
        c.wait()


def make_z(where, m, w):
    g = m.shape[1]
    shape = jax.ShapeDtypeStruct((2, 192, g), F32)
    return pl.pallas_call(
        z_kernel,
        in_specs=[SMEM] + [ANY] * 7,
        out_specs=[ANY, ANY],
        out_shape=[shape, shape],
        scratch_shapes=[
            pltpu.VMEM((768, g), BF16),
            pltpu.VMEM((g, g), BF16),
            pltpu.VMEM((4, 192, g), F32),
            pltpu.SemaphoreType.DMA((16,)),
            pltpu.SemaphoreType.DMA((8,)),
            pltpu.SemaphoreType.DMA((4,)),
        ],
        compiler_params=pltpu.CompilerParams(vmem_limit_bytes=VMEM_LIMIT),
        cost_estimate=pl.CostEstimate(flops=2 * 768 * g * g, bytes_accessed=40000000, transcendentals=0),
        name="make_z",
    )(where, m, *w)


def last_kernel(where, *refs):
    z, mx = blocks_of(refs[0:6]), refs[6:12]
    out, zs, xs, total, sem = refs[12:]
    x, zl, y = where[0], where[1], where[2]
    thirds = [[], [], []]
    for third in range(3):
        part = pl.ds(2 * third, 2)
        for at in range(8):
            thirds[third].append(pltpu.make_async_copy(z[at].at[part], zs.at[part, at], sem.at[third, at]))
        for j in (0, 2):
            to = xs.at[part, (x + 4 - j) % 4]
            thirds[third].append(pltpu.make_async_copy(mx[j // 2].at[part], to, sem.at[third, 8 + j]))
        for j in (1, 3):
            to = (x + 4 - j) % 4
            for w in range(2 * third, 2 * third + 2):
                own = mx[j + 1 + w // 3].at[w % 3]
                thirds[third].append(pltpu.make_async_copy(own, xs.at[w, to], sem.at[third, 8 + j + 4 * (w % 2)]))
        for c in thirds[third]:
            c.start()
    sums = jnp.zeros((256, 256), F32)
    for third in range(3):
        for c in thirds[third]:
            c.wait()
        for w in range(2 * third, 2 * third + 2):
            lhs = zs[w].reshape(256, zs.shape[3])
            rhs = xs[w].reshape(256, xs.shape[3])
            sums = sums + lax.dot_general(lhs, rhs, NT, preferred_element_type=F32)
    for z_of in range(2):
        for y_of in range(4):
            to = ((zl + z_of) % 2 * 4 + (y + y_of) % 4) * 8
            for r in range(4):
                at = ((z_of * 4 + y_of) * 4 + r) * 8
                total[pl.ds(pl.multiple_of(r * 64 + to, 8), 8), :] = sums[at : at + 8]
    turned = total[...].T
    for j in range(4):
        for p in range(4):
            cols = slice(64 * p, 64 * p + 64)
            halves = [turned[64 * j + at : 64 * j + at + 32, cols] for at in (0, 32)]
            out[4 * j + p] = jnp.concatenate(halves, axis=1)


def last(where, z, mixed):
    g = mixed[0].shape[2]
    return pl.pallas_call(
        last_kernel,
        in_specs=[SMEM] + [ANY] * 12,
        out_specs=VMEM,
        out_shape=jax.ShapeDtypeStruct((16, 32, 128), F32),
        scratch_shapes=[
            pltpu.VMEM((6, 8, 32, g), BF16),
            pltpu.VMEM((6, 4, 64, g), BF16),
            pltpu.VMEM((256, 256), F32),
            pltpu.SemaphoreType.DMA((3, 16)),
        ],
        compiler_params=pltpu.CompilerParams(vmem_limit_bytes=VMEM_LIMIT),
        cost_estimate=pl.CostEstimate(flops=2 * 256 * 256 * 6 * g, bytes_accessed=8000000, transcendentals=0),
        name="last",
    )(where, *z, *mixed)


def shards(cond_pairs, vectors, screened, val_pairs):
    g = cond_pairs.shape[2]
    axes = ("x", "zl", "y", "zh", "core")
    where = jnp.stack([lax.axis_index(a) for a in axes]).astype(jnp.int32)

    own = jnp.transpose(vectors, (2, 1, 0)).reshape(8, 192)
    line = [own] + [shift_from(own, "y", s) for s in (1, 2, 3)]
    line, screened_far = lax.optimization_barrier((line, screened))
    lines = jnp.broadcast_to(jnp.concatenate(line)[None], (8, 32, 192))

    w_own = screened_far.T
    other, two = swap(screened.T, "zl"), shift_from(w_own, "y", 2)

    m_own = jnp.transpose(val_pairs, (1, 0, 2)).reshape(192, g)
    m = lax.all_gather(m_own, "x", axis=0, tiled=True)

    x_all = lax.all_to_all(lines, ("x", "zl"), split_axis=0, concat_axis=0, tiled=True).reshape(256, 192)
    other, two, x_all = lax.optimization_barrier((other, two, x_all))
    w = end_gather(w_own, other, two)

    mixed = mix(where, x_all, cond_pairs)
    mixed = list(mixed)
    w[3], mixed[2], mixed[4] = lax.optimization_barrier((w[3], mixed[2], mixed[4]))
    m, w, mixed[0] = lax.optimization_barrier((m, w, mixed[0]))
    mixed[2], mixed[4] = shift_to(mixed[2], "x", 1), shift_to(mixed[4], "x", 3)

    send, keep = make_z(where, m, w)
    send, keep, mixed = lax.optimization_barrier((send, keep, mixed))
    got = swap(send, "core")
    part = [(keep[a] + got[a]).astype(BF16) for a in range(2)]
    got = []
    for a in range(2):
        perm = [
            (x * 4 + zh * 2 + c, (2 * c + (zh ^ a)) * 4 + x) for x in range(4) for zh in range(2) for c in range(2)
        ]
        got.append(lax.ppermute(part[a], ("x", "zh", "core"), perm))
    got, mixed = lax.optimization_barrier((got, mixed))
    z_own = (got[0].astype(F32) + got[1].astype(F32)).astype(BF16).reshape(6, 32, g)
    other, two = swap(z_own, "zl"), shift_from(z_own, "y", 2)
    mixed[3], mixed[5] = shift_to(mixed[3], "x", 1), shift_to(mixed[5], "x", 3)
    z_own, other, two = lax.optimization_barrier((z_own, other, two))
    mixed = lax.optimization_barrier(mixed)
    z = end_gather(z_own, other, two)
    mixed[1] = shift_to(mixed[1], "x", 2)

    sums = last(where, z, mixed)
    sums = lax.all_to_all(sums, ("x", "zh", "core"), split_axis=0, concat_axis=0, tiled=True)
    total = jnp.sum(sums, axis=0)
    total = jnp.stack([total[:, :64], total[:, 64:]])
    return jnp.transpose(total.reshape(8, 8, 64), (1, 2, 0))


def solution(mesh):
    fine = Mesh(mesh.devices.reshape(4, 2, 4, 2, 2), ("x", "zl", "y", "zh", "core"))
    band, pw = ("x", "zl", "y"), ("zh", "core")
    return jax.shard_map(
        shards,
        mesh=fine,
        in_specs=(P(band, None, pw), P(None, None, band), P(pw, band), P(band, None, pw)),
        out_specs=P(None, pw, band),
        check_vma=False,
    )
```

```python
import jax
import jax.numpy as jnp
from jax import lax
from jax.experimental import pallas as pl
from jax.experimental.pallas import tpu as pltpu
from jax.sharding import Mesh, PartitionSpec as P

F32, BF16 = jnp.float32, jnp.bfloat16
ANY = pl.BlockSpec(memory_space=pl.ANY)
SMEM = pl.BlockSpec(memory_space=pltpu.SMEM)
VMEM = pl.BlockSpec(memory_space=pltpu.VMEM)
VMEM_LIMIT = 60 * 1024 * 1024

NX, NY = 4, 4
NT = (((1,), (1,)), ((), ()))


def shift_from(a, axis, s):
    return lax.ppermute(a, axis, [(i, (i - s) % 4) for i in range(4)])


def shift_to(a, axis, s):
    return lax.ppermute(a, axis, [(i, (i + s) % 4) for i in range(4)])


def swap(a, axis):
    return lax.ppermute(a, axis, [(0, 1), (1, 0)])


def end_gather(own, other, two):
    pair = jnp.stack([own, other])
    return [own, other, two, swap(two, "zl"), shift_from(pair, "y", 1), shift_from(pair, "y", 3)]


def blocks_of(refs):
    own, other, two, other_two, one, three = refs
    return [own, one.at[0], two, three.at[0], other, one.at[1], other_two, three.at[1]]


def mixed_kernel(where, x_ref, b_ref, *refs):
    outs, xs, rows, square = refs[:6], refs[6], refs[7], refs[8]

    @pl.when(pl.program_id(0) == 0)
    def _():
        x, y = where[0], where[2]
        given = x_ref[...].astype(F32)
        for at in range(32):
            to = at // 4 * 32 + (y + at % 4) % 4 * 8
            square[pl.ds(pl.multiple_of(to, 8), 8), :] = given[at * 8 : at * 8 + 8]
        rows[...] = square[...].T
        for j in range(4):
            q = (x + j) % 4
            xs[j * 48 : j * 48 + 48, :] = rows[pl.ds(pl.multiple_of(q * 48, 48), 48), :].astype(BF16)

    lhs = xs[...]
    for n in range(b_ref.shape[2] // 256):
        cols = slice(256 * n, 256 * n + 256)
        two = [jnp.dot(lhs, b_ref[i, :, cols], preferred_element_type=F32) for i in range(2)]
        for j in range(4):
            for w in range(6):
                at = (j * 6 + w) * 8
                both = jnp.concatenate([t[at : at + 8] for t in two], axis=0)
                if j % 2:
                    outs[j + 1 + w // 3][w % 3, :, cols] = both.astype(BF16)
                else:
                    outs[j // 2][w, :, cols] = both.astype(BF16)


def mix(where, x_all, cond):
    g = cond.shape[2]
    return pl.pallas_call(
        mixed_kernel,
        grid=(4,),
        in_specs=[
            SMEM,
            pl.BlockSpec((256, 192), lambda i: (0, 0)),
            pl.BlockSpec((2, 256, g), lambda i: (i, 0, 0)),
        ],
        out_specs=[pl.BlockSpec((6, 16, g), lambda i: (0, i, 0))] * 2
        + [pl.BlockSpec((n, 16, g), lambda i: (0, i, 0)) for n in (3, 3, 3, 3)],
        out_shape=[jax.ShapeDtypeStruct((n, 64, g), BF16) for n in (6, 6, 3, 3, 3, 3)],
        scratch_shapes=[pltpu.VMEM((192, 256), BF16), pltpu.VMEM((192, 256), F32), pltpu.VMEM((256, 192), F32)],
        compiler_params=pltpu.CompilerParams(vmem_limit_bytes=VMEM_LIMIT),
        cost_estimate=pl.CostEstimate(flops=2 * 192 * 256 * 8 * g, bytes_accessed=9200000, transcendentals=0),
        name="mix",
    )(where, x_all, cond)


def z_kernel(where, m, *refs):
    w = blocks_of(refs[0:6])
    send, keep, ms, ws, sums_send, sums_keep, m_sem, w_sem, out_sem = refs[6:]
    sums = [sums_send, sums_keep]
    zl, y, zh, core = where[1], where[2], where[3], where[4]
    copies = []
    for t in range(4):
        owner = 1 - core if t < 2 else core
        q = 2 * owner + (zh + t % 2) % 2
        for r in range(4):
            to = ms.at[pl.ds((t * 4 + r) * 48, 48)]
            at = pl.ds(pl.multiple_of(192 * r + q * 48, 48), 48)
            copies.append(pltpu.make_async_copy(m.at[at], to, m_sem.at[t * 4 + r]))
    for c in copies:
        c.start()
    for at in range(8):
        to = (zl + at // 4) % 2 * 4 + (y + at % 4) % 4
        pltpu.make_async_copy(w[at], ws.at[pl.ds(pl.multiple_of(to * 160, 160), 160)], w_sem.at[to]).start()
    for c in copies:
        c.wait()

    for i in range(8):
        pltpu.make_async_copy(w[0], ws.at[pl.ds(i * 160, 160)], w_sem.at[i]).wait()
    outs = []
    for half, out in enumerate((send, keep)):
        res = lax.dot_general(ms[384 * half : 384 * half + 384, :], ws[...], NT, preferred_element_type=F32)
        for a in range(2):
            for k in range(6):
                rows = [((a * 4 + r) * 6 + k) * 8 for r in range(4)]
                block = jnp.concatenate([res[at : at + 8] for at in rows], axis=0)
                sums[half][a, 32 * k : 32 * k + 32, :] = block.astype(out.dtype)
            outs.append(pltpu.make_async_copy(sums[half].at[a], out.at[a], out_sem.at[2 * half + a]))
            outs[-1].start()
    for c in outs:
        c.wait()


def make_z(where, m, w):
    g = m.shape[1]
    return pl.pallas_call(
        z_kernel,
        in_specs=[SMEM] + [ANY] * 7,
        out_specs=[ANY, ANY],
        out_shape=[jax.ShapeDtypeStruct((2, 192, g), kind) for kind in (BF16, F32)],
        scratch_shapes=[
            pltpu.VMEM((768, g), BF16),
            pltpu.VMEM((g, g), BF16),
            pltpu.VMEM((2, 192, g), BF16),
            pltpu.VMEM((2, 192, g), F32),
            pltpu.SemaphoreType.DMA((16,)),
            pltpu.SemaphoreType.DMA((8,)),
            pltpu.SemaphoreType.DMA((4,)),
        ],
        compiler_params=pltpu.CompilerParams(vmem_limit_bytes=VMEM_LIMIT),
        cost_estimate=pl.CostEstimate(flops=2 * 768 * g * g, bytes_accessed=40000000, transcendentals=0),
        name="make_z",
    )(where, m, *w)


def last_kernel(where, *refs):
    z, mx = blocks_of(refs[0:6]), refs[6:12]
    out, zs, xs, total, sem = refs[12:]
    x, zl, y = where[0], where[1], where[2]
    thirds = [[], [], []]
    for third in range(3):
        part = pl.ds(2 * third, 2)
        for at in range(8):
            thirds[third].append(pltpu.make_async_copy(z[at].at[part], zs.at[part, at], sem.at[third, at]))
        for j in (0, 2):
            to = xs.at[part, (x + 4 - j) % 4]
            thirds[third].append(pltpu.make_async_copy(mx[j // 2].at[part], to, sem.at[third, 8 + j]))
        for j in (1, 3):
            to = (x + 4 - j) % 4
            for w in range(2 * third, 2 * third + 2):
                own = mx[j + 1 + w // 3].at[w % 3]
                thirds[third].append(pltpu.make_async_copy(own, xs.at[w, to], sem.at[third, 8 + j + 4 * (w % 2)]))
        for c in thirds[third]:
            c.start()
    sums = jnp.zeros((256, 256), F32)
    for third in range(3):
        for c in thirds[third]:
            c.wait()
        for w in range(2 * third, 2 * third + 2):
            lhs = zs[w].reshape(256, zs.shape[3])
            rhs = xs[w].reshape(256, xs.shape[3])
            sums = sums + lax.dot_general(lhs, rhs, NT, preferred_element_type=F32)
    for z_of in range(2):
        for y_of in range(4):
            to = ((zl + z_of) % 2 * 4 + (y + y_of) % 4) * 8
            for r in range(4):
                at = ((z_of * 4 + y_of) * 4 + r) * 8
                total[pl.ds(pl.multiple_of(r * 64 + to, 8), 8), :] = sums[at : at + 8]
    turned = total[...].T
    for j in range(4):
        for p in range(4):
            cols = slice(64 * p, 64 * p + 64)
            halves = [turned[64 * j + at : 64 * j + at + 32, cols] for at in (0, 32)]
            out[4 * j + p] = jnp.concatenate(halves, axis=1)


def last(where, z, mixed):
    g = mixed[0].shape[2]
    return pl.pallas_call(
        last_kernel,
        in_specs=[SMEM] + [ANY] * 12,
        out_specs=VMEM,
        out_shape=jax.ShapeDtypeStruct((16, 32, 128), F32),
        scratch_shapes=[
            pltpu.VMEM((6, 8, 32, g), BF16),
            pltpu.VMEM((6, 4, 64, g), BF16),
            pltpu.VMEM((256, 256), F32),
            pltpu.SemaphoreType.DMA((3, 16)),
        ],
        compiler_params=pltpu.CompilerParams(vmem_limit_bytes=VMEM_LIMIT),
        cost_estimate=pl.CostEstimate(flops=2 * 256 * 256 * 6 * g, bytes_accessed=8000000, transcendentals=0),
        name="last",
    )(where, *z, *mixed)


def shards(cond_pairs, vectors, screened, val_pairs):
    g = cond_pairs.shape[2]
    axes = ("x", "zl", "y", "zh", "core")
    where = jnp.stack([lax.axis_index(a) for a in axes]).astype(jnp.int32)

    own = jnp.transpose(vectors, (2, 1, 0)).reshape(8, 192)
    line = [own] + [shift_from(own, "y", s) for s in (1, 2, 3)]
    line, screened_far = lax.optimization_barrier((line, screened))
    lines = jnp.broadcast_to(jnp.concatenate(line)[None], (8, 32, 192))

    w_own = screened_far.T
    other, two = swap(screened.T, "zl"), shift_from(w_own, "y", 2)

    m_own = jnp.transpose(val_pairs, (1, 0, 2)).reshape(192, g)
    m = lax.all_gather(m_own, "x", axis=0, tiled=True)

    x_all = lax.all_to_all(lines, ("x", "zl"), split_axis=0, concat_axis=0, tiled=True).reshape(256, 192)
    other, two, x_all = lax.optimization_barrier((other, two, x_all))
    w = end_gather(w_own, other, two)

    mixed = mix(where, x_all, cond_pairs)
    mixed = list(mixed)
    w[3], mixed[2], mixed[4] = lax.optimization_barrier((w[3], mixed[2], mixed[4]))
    m, w, mixed[0] = lax.optimization_barrier((m, w, mixed[0]))
    mixed[2], mixed[4] = shift_to(mixed[2], "x", 1), shift_to(mixed[4], "x", 3)

    send, keep = make_z(where, m, w)
    send, keep, mixed = lax.optimization_barrier((send, keep, mixed))
    got = swap(send, "core")
    part = [(keep[a] + got[a].astype(F32)).astype(BF16) for a in range(2)]
    got = []
    for a in range(2):
        perm = [
            (x * 4 + zh * 2 + c, (2 * c + (zh ^ a)) * 4 + x) for x in range(4) for zh in range(2) for c in range(2)
        ]
        got.append(lax.ppermute(part[a], ("x", "zh", "core"), perm))
    got, mixed = lax.optimization_barrier((got, mixed))
    z_own = (got[0].astype(F32) + got[1].astype(F32)).astype(BF16).reshape(6, 32, g)
    other, two = swap(z_own, "zl"), shift_from(z_own, "y", 2)
    mixed[3], mixed[5] = shift_to(mixed[3], "x", 1), shift_to(mixed[5], "x", 3)
    z_own, other, two = lax.optimization_barrier((z_own, other, two))
    mixed = lax.optimization_barrier(mixed)
    z = end_gather(z_own, other, two)
    mixed[1] = shift_to(mixed[1], "x", 2)

    sums = last(where, z, mixed)
    sums = lax.all_to_all(sums, ("x", "zh", "core"), split_axis=0, concat_axis=0, tiled=True)
    total = jnp.sum(sums, axis=0)
    total = jnp.stack([total[:, :64], total[:, 64:]])
    return jnp.transpose(total.reshape(8, 8, 64), (1, 2, 0))


def solution(mesh):
    fine = Mesh(mesh.devices.reshape(4, 2, 4, 2, 2), ("x", "zl", "y", "zh", "core"))
    band, pw = ("x", "zl", "y"), ("zh", "core")
    return jax.shard_map(
        shards,
        mesh=fine,
        in_specs=(P(band, None, pw), P(None, None, band), P(pw, band), P(band, None, pw)),
        out_specs=P(None, pw, band),
        check_vma=False,
    )
```

```python
import jax
import jax.numpy as jnp
from jax import lax
from jax.experimental import pallas as pl
from jax.experimental.pallas import tpu as pltpu
from jax.sharding import Mesh, PartitionSpec as P

F32, BF16 = jnp.float32, jnp.bfloat16
ANY = pl.BlockSpec(memory_space=pl.ANY)
SMEM = pl.BlockSpec(memory_space=pltpu.SMEM)
VMEM = pl.BlockSpec(memory_space=pltpu.VMEM)
VMEM_LIMIT = 60 * 1024 * 1024

NX, NY = 4, 4
NT = (((1,), (1,)), ((), ()))


def shift_from(a, axis, s):
    return lax.ppermute(a, axis, [(i, (i - s) % 4) for i in range(4)])


def shift_to(a, axis, s):
    return lax.ppermute(a, axis, [(i, (i + s) % 4) for i in range(4)])


def swap(a, axis):
    return lax.ppermute(a, axis, [(0, 1), (1, 0)])


def end_gather(own, other, two):
    pair = jnp.stack([own, other])
    return [own, other, two, swap(two, "zl"), shift_from(pair, "y", 1), shift_from(pair, "y", 3)]


def blocks_of(refs):
    own, other, two, other_two, one, three = refs
    return [own, one.at[0], two, three.at[0], other, one.at[1], other_two, three.at[1]]


def mixed_kernel(where, x_ref, b_ref, *refs):
    outs, xs, rows, square = refs[:6], refs[6], refs[7], refs[8]

    @pl.when(pl.program_id(0) == 0)
    def _():
        x, y = where[0], where[2]
        given = x_ref[...].astype(F32)
        for at in range(32):
            to = at // 4 * 32 + (y + at % 4) % 4 * 8
            square[pl.ds(pl.multiple_of(to, 8), 8), :] = given[at * 8 : at * 8 + 8]
        rows[...] = square[...].T
        for j in range(4):
            q = (x + j) % 4
            xs[j * 48 : j * 48 + 48, :] = rows[pl.ds(pl.multiple_of(q * 48, 48), 48), :].astype(BF16)

    lhs = xs[...]
    for n in range(b_ref.shape[2] // 256):
        cols = slice(256 * n, 256 * n + 256)
        two = [jnp.dot(lhs, b_ref[i, :, cols], preferred_element_type=F32) for i in range(2)]
        for j in range(4):
            for w in range(6):
                at = (j * 6 + w) * 8
                both = jnp.concatenate([t[at : at + 8] for t in two], axis=0)
                if j % 2:
                    outs[j + 1 + w // 3][w % 3, :, cols] = both.astype(BF16)
                else:
                    outs[j // 2][w, :, cols] = both.astype(BF16)


def mix(where, x_all, cond):
    g = cond.shape[2]
    return pl.pallas_call(
        mixed_kernel,
        grid=(4,),
        in_specs=[
            SMEM,
            pl.BlockSpec((256, 192), lambda i: (0, 0)),
            pl.BlockSpec((2, 256, g), lambda i: (i, 0, 0)),
        ],
        out_specs=[pl.BlockSpec((6, 16, g), lambda i: (0, i, 0))] * 2
        + [pl.BlockSpec((n, 16, g), lambda i: (0, i, 0)) for n in (3, 3, 3, 3)],
        out_shape=[jax.ShapeDtypeStruct((n, 64, g), BF16) for n in (6, 6, 3, 3, 3, 3)],
        scratch_shapes=[pltpu.VMEM((192, 256), BF16), pltpu.VMEM((192, 256), F32), pltpu.VMEM((256, 192), F32)],
        compiler_params=pltpu.CompilerParams(vmem_limit_bytes=VMEM_LIMIT),
        cost_estimate=pl.CostEstimate(flops=2 * 192 * 256 * 8 * g, bytes_accessed=9200000, transcendentals=0),
        name="mix",
    )(where, x_all, cond)


def z_kernel(where, m, *refs):
    w = blocks_of(refs[0:6])
    send, keep, ms, ws, sums, m_sem, w_sem, out_sem = refs[6:]
    zl, y, zh, core = where[1], where[2], where[3], where[4]
    copies = []
    for t in range(4):
        owner = 1 - core if t < 2 else core
        q = 2 * owner + (zh + t % 2) % 2
        for r in range(4):
            to = ms.at[pl.ds((t * 4 + r) * 48, 48)]
            at = pl.ds(pl.multiple_of(192 * r + q * 48, 48), 48)
            copies.append(pltpu.make_async_copy(m.at[at], to, m_sem.at[t * 4 + r]))
    for c in copies:
        c.start()
    for at in range(8):
        to = (zl + at // 4) % 2 * 4 + (y + at % 4) % 4
        pltpu.make_async_copy(w[at], ws.at[pl.ds(pl.multiple_of(to * 160, 160), 160)], w_sem.at[to]).start()
    for c in copies:
        c.wait()

    for i in range(8):
        pltpu.make_async_copy(w[0], ws.at[pl.ds(i * 160, 160)], w_sem.at[i]).wait()
    outs = []
    for half, out in enumerate((send, keep)):
        res = lax.dot_general(ms[384 * half : 384 * half + 384, :], ws[...], NT, preferred_element_type=F32)
        for a in range(2):
            t = 2 * half + a
            for k in range(6):
                for r in range(4):
                    at = ((a * 4 + r) * 6 + k) * 8
                    sums[t, (k * 4 + r) * 8 : (k * 4 + r) * 8 + 8, :] = res[at : at + 8]
            outs.append(pltpu.make_async_copy(sums.at[t], out.at[a], out_sem.at[t]))
            outs[-1].start()
    for c in outs:
        c.wait()


def make_z(where, m, w):
    g = m.shape[1]
    shape = jax.ShapeDtypeStruct((2, 192, g), F32)
    return pl.pallas_call(
        z_kernel,
        in_specs=[SMEM] + [ANY] * 7,
        out_specs=[ANY, ANY],
        out_shape=[shape, shape],
        scratch_shapes=[
            pltpu.VMEM((768, g), BF16),
            pltpu.VMEM((g, g), BF16),
            pltpu.VMEM((4, 192, g), F32),
            pltpu.SemaphoreType.DMA((16,)),
            pltpu.SemaphoreType.DMA((8,)),
            pltpu.SemaphoreType.DMA((4,)),
        ],
        compiler_params=pltpu.CompilerParams(vmem_limit_bytes=VMEM_LIMIT),
        cost_estimate=pl.CostEstimate(flops=2 * 768 * g * g, bytes_accessed=40000000, transcendentals=0),
        name="make_z",
    )(where, m, *w)


def last_kernel(where, *refs):
    z, mx = blocks_of(refs[0:6]), refs[6:12]
    out, zs, xs, total, sem = refs[12:]
    x, zl, y = where[0], where[1], where[2]
    thirds = [[], [], []]
    for third in range(3):
        part = pl.ds(2 * third, 2)
        for at in range(8):
            thirds[third].append(pltpu.make_async_copy(z[at].at[part], zs.at[part, at], sem.at[third, at]))
        for j in (0, 2):
            to = xs.at[part, (x + 4 - j) % 4]
            thirds[third].append(pltpu.make_async_copy(mx[j // 2].at[part], to, sem.at[third, 8 + j]))
        for j in (1, 3):
            to = (x + 4 - j) % 4
            for w in range(2 * third, 2 * third + 2):
                own = mx[j + 1 + w // 3].at[w % 3]
                thirds[third].append(pltpu.make_async_copy(own, xs.at[w, to], sem.at[third, 8 + j + 4 * (w % 2)]))
        for c in thirds[third]:
            c.start()
    sums = jnp.zeros((256, 256), F32)
    for third in range(3):
        for c in thirds[third]:
            c.wait()
        for w in range(2 * third, 2 * third + 2):
            lhs = zs[w].reshape(256, zs.shape[3])
            rhs = xs[w].reshape(256, xs.shape[3])
            sums = sums + lax.dot_general(lhs, rhs, NT, preferred_element_type=F32)
    for z_of in range(2):
        for y_of in range(4):
            to = ((zl + z_of) % 2 * 4 + (y + y_of) % 4) * 8
            for r in range(4):
                at = ((z_of * 4 + y_of) * 4 + r) * 8
                total[pl.ds(pl.multiple_of(r * 64 + to, 8), 8), :] = sums[at : at + 8]
    turned = total[...].T
    for j in range(4):
        for p in range(4):
            cols = slice(64 * p, 64 * p + 64)
            halves = [turned[64 * j + at : 64 * j + at + 32, cols] for at in (0, 32)]
            out[4 * j + p] = jnp.concatenate(halves, axis=1)


def last(where, z, mixed):
    g = mixed[0].shape[2]
    return pl.pallas_call(
        last_kernel,
        in_specs=[SMEM] + [ANY] * 12,
        out_specs=VMEM,
        out_shape=jax.ShapeDtypeStruct((16, 32, 128), F32),
        scratch_shapes=[
            pltpu.VMEM((6, 8, 32, g), BF16),
            pltpu.VMEM((6, 4, 64, g), BF16),
            pltpu.VMEM((256, 256), F32),
            pltpu.SemaphoreType.DMA((3, 16)),
        ],
        compiler_params=pltpu.CompilerParams(vmem_limit_bytes=VMEM_LIMIT),
        cost_estimate=pl.CostEstimate(flops=2 * 256 * 256 * 6 * g, bytes_accessed=8000000, transcendentals=0),
        name="last",
    )(where, *z, *mixed)


def shards(cond_pairs, vectors, screened, val_pairs):
    g = cond_pairs.shape[2]
    axes = ("x", "zl", "y", "zh", "core")
    where = jnp.stack([lax.axis_index(a) for a in axes]).astype(jnp.int32)

    own = jnp.transpose(vectors, (2, 1, 0)).reshape(8, 192)
    line = [own] + [shift_from(own, "y", s) for s in (1, 2, 3)]
    line, screened_far = lax.optimization_barrier((line, screened))
    lines = jnp.broadcast_to(jnp.concatenate(line)[None], (8, 32, 192))

    w_own = screened_far.T
    other, two = swap(screened.T, "zl"), shift_from(w_own, "y", 2)

    m_own = jnp.transpose(val_pairs, (1, 0, 2)).reshape(192, g)
    m = lax.all_gather(m_own, "x", axis=0, tiled=True)

    x_all = lax.all_to_all(lines, ("x", "zl"), split_axis=0, concat_axis=0, tiled=True).reshape(256, 192)
    other, two, x_all = lax.optimization_barrier((other, two, x_all))
    w = end_gather(w_own, other, two)

    mixed = mix(where, x_all, cond_pairs)
    mixed = list(mixed)
    w[3], mixed[2], mixed[4] = lax.optimization_barrier((w[3], mixed[2], mixed[4]))
    m, w, mixed[0] = lax.optimization_barrier((m, w, mixed[0]))
    mixed[2], mixed[4] = shift_to(mixed[2], "x", 1), shift_to(mixed[4], "x", 3)

    send, keep = make_z(where, m, w)
    send, keep, mixed = lax.optimization_barrier((send, keep, mixed))
    got = swap(send, "core")
    part = [(keep[a] + got[a]).astype(BF16) for a in range(2)]
    got = []
    for a in range(2):
        perm = [
            (x * 4 + zh * 2 + c, (2 * c + (zh ^ a)) * 4 + x) for x in range(4) for zh in range(2) for c in range(2)
        ]
        got.append(lax.ppermute(part[a], ("x", "zh", "core"), perm))
    got, mixed = lax.optimization_barrier((got, mixed))
    z_own = (got[0].astype(F32) + got[1].astype(F32)).astype(BF16).reshape(6, 32, g)
    other, two = swap(z_own, "zl"), shift_from(z_own, "y", 2)
    mixed[1] = shift_to(mixed[1], "x", 2)
    mixed = lax.optimization_barrier(mixed)
    mixed[3], mixed[5] = shift_to(mixed[3], "x", 1), shift_to(mixed[5], "x", 3)
    z_own, other, two = lax.optimization_barrier((z_own, other, two))
    z = end_gather(z_own, other, two)

    sums = last(where, z, mixed)
    sums = lax.all_to_all(sums, ("x", "zh", "core"), split_axis=0, concat_axis=0, tiled=True)
    total = jnp.sum(sums, axis=0)
    total = jnp.stack([total[:, :64], total[:, 64:]])
    return jnp.transpose(total.reshape(8, 8, 64), (1, 2, 0))


def solution(mesh):
    fine = Mesh(mesh.devices.reshape(4, 2, 4, 2, 2), ("x", "zl", "y", "zh", "core"))
    band, pw = ("x", "zl", "y"), ("zh", "core")
    return jax.shard_map(
        shards,
        mesh=fine,
        in_specs=(P(band, None, pw), P(None, None, band), P(pw, band), P(band, None, pw)),
        out_specs=P(None, pw, band),
        check_vma=False,
    )
```
